256 devices in a mesh: dp: 4 (over x), ctx: 64 (over z, y, core).
Axes of the slice: x: 4, y: 4, z: 8, core: 2. Of those that a mesh axis runs over, the one named last changes fastest.
Arguments:
- saved_pre: bfloat16 [32768, 8, 1024], P(('dp', 'ctx')), may hold values from -6 to 6
- layer_grad: bfloat16 [32768, 2304], P(('dp', 'ctx')), may hold values from -4 to 4
- router_weight: bfloat16 [32768, 8], P(('dp', 'ctx')), may hold values from 0.049804688 to 0.5
- routes: int32 [32768, 8], P(('dp', 'ctx')), may hold values from 0 to 127, all different within a row; in each aligned block of 128 rows (0 to 127, 128 to 255, ...) at most 9 rows name the same one
- queries: bfloat16 [4, 8192, 1024], P('dp', 'ctx'), may hold values from -0.625 to 0.625
- key_vectors: bfloat16 [4, 8192, 1024], P('dp', 'ctx'), may hold values from -2 to 2
- value_vectors: bfloat16 [4, 8192, 1024], P('dp', 'ctx'), may hold values from -2 to 2
- head_grad: bfloat16 [4, 8192, 1024], P('dp', 'ctx'), may hold values from -6 to 6
- log_gate: float32 [4, 8192, 1024], P('dp', 'ctx'), may hold values from -1 to 0
Outputs:
- key_grad: bfloat16 [4, 8192, 1024], P('dp', 'ctx')
- value_grad: bfloat16 [4, 8192, 1024], P('dp', 'ctx')
- down_grad: bfloat16 [128, 512, 2304], P('ctx', None, 'dp')
The draws below stay inside these ranges and needn't reach their ends.
Inputs may be any that keep to these rules, and one draw needn't show every extreme that they name: `routes`: within the rows of one device each expert is named by at most 9 rows, a bound that some block reaches; each row names 8 different experts.
All inputs are finite; a program needn't handle non-finite values.
Results may differ from the reference program's by a relative error of at most 0.0057.
Values may be sent and summed in bfloat16 or wider, within the bound.
A program may use at most 192 MiB of HBM per device.

```python
import math
import jax
import jax.numpy as jnp
import numpy as np
from jax import lax

D = 2304
FF = 512
HEADS = 16
HEAD_K = 64
TOP = 8
TOK_DEV = 128
EXPERTS = 128
CAP = 9
DATA_GROUPS = 4
SEQUENCE_TOKENS = 8192
ROWS = 32768


def draw_log_gate(key, part):
    key = jax.random.fold_in(key, 7)
    piece_count = jax.random.split(key, 7)
    width = HEADS * HEAD_K
    blocks = SEQUENCE_TOKENS // TOK_DEV
    fast_share = 0.5
    coarse_estimate = jnp.clip(1.0 + 0.3 * jax.random.normal(piece_count[5], (DATA_GROUPS, SEQUENCE_TOKENS, width), jnp.float32), 0.5, 1.5)
    fast = jax.random.uniform(piece_count[0], (DATA_GROUPS, 1, width)) < fast_share
    slow_rate = jnp.exp(jax.random.uniform(piece_count[1], (DATA_GROUPS, 1, width), jnp.float32, math.log(0.15), math.log(0.3))) / SEQUENCE_TOKENS
    fast_rate = jax.random.uniform(piece_count[2], (DATA_GROUPS, 1, width), jnp.float32, 1.0 / 50.0, 1.0 / 30.0)
    decay_speed = jnp.where(fast, fast_rate, slow_rate)
    replica_multiplier = jnp.exp(jax.random.uniform(piece_count[3], (DATA_GROUPS, blocks, 1, width), jnp.float32, -0.35, 0.35))
    replica_multiplier = jnp.broadcast_to(replica_multiplier, (DATA_GROUPS, blocks, TOK_DEV, width)).reshape(DATA_GROUPS, SEQUENCE_TOKENS, width)
    spike_position = jax.random.randint(piece_count[4], (DATA_GROUPS, 2), 0, SEQUENCE_TOKENS)
    token_position = jnp.arange(SEQUENCE_TOKENS)[None, :]
    spike_mask = ((token_position == spike_position[:, 0:1]) | (token_position == spike_position[:, 1:2])).astype(jnp.float32)[:, :, None]
    layer_depth = jax.random.uniform(piece_count[6], (DATA_GROUPS, 1, width), jnp.float32, math.log(0.5), math.log(0.8))
    return (-decay_speed * replica_multiplier * coarse_estimate + spike_mask * layer_depth).astype(jnp.float32)


def level_of(stream_key, dims, shards, low, high):
    def one(axis_at, shards_of):
        draws = jax.random.uniform(jax.random.fold_in(jax.random.fold_in(stream_key, 6), axis_at), (shards_of,), jnp.float32, low / len(shards), high / len(shards))
        return jnp.repeat(jnp.exp(draws), dims[axis_at] // shards_of).reshape((-1,) + (1,) * (len(dims) - axis_at - 1))

    loudness = one(*shards[0])
    for cut in shards[1:]:
        loudness = loudness * one(*cut)
    return loudness


def deal_out(rng, own, number, rows, count, top, bound, slope):
    sequence = jax.random.permutation(rng, count)
    heavy_load, ordinary = load_shares(count, rows * top, bound, slope, True), load_shares(count, rows * top, bound, slope, False)
    places = jnp.arange(count)

    def named(lengths, offset_by):
        used = int((lengths > 0).sum())
        fixed = max(1, used // 4)
        moved = fixed + (places - fixed + offset_by * (used - fixed)) % max(1, count - fixed)
        return jnp.zeros((count,), jnp.int32).at[sequence[jnp.where(places < fixed, places, moved)]].set(jnp.asarray(lengths, jnp.int32))

    lengths = jnp.where(number % 4 == 0, named(heavy_load, number // 4), named(ordinary, number - number // 4 - 1))
    mixed = jax.random.permutation(jax.random.fold_in(own, 3), count)
    donor, sink = mixed[0:count // 2 * 2:2], mixed[1:count // 2 * 2:2]
    room = jnp.minimum(lengths[donor] - 1, bound - lengths[sink]) // 2
    room = jnp.where((donor == sequence[0]) | (sink == sequence[0]) | (lengths[sink] == 0), 0, jnp.maximum(room, 0))
    moved = jax.random.randint(jax.random.fold_in(own, 4), (count // 2,), 0, 1 << 20) % (room + 1)
    lengths = lengths.at[donor].add(-moved).at[sink].add(moved)
    members = jnp.searchsorted(jnp.cumsum(lengths), jnp.arange(rows * top), side="right").astype(jnp.int32)
    table = members.reshape(top, rows).T
    table = table[jax.random.permutation(jax.random.fold_in(own, 1), rows)]
    offset_by = jax.random.randint(jax.random.fold_in(own, 2), (rows, 1), 0, top)
    return jnp.take_along_axis(table, (jnp.arange(top)[None, :] + offset_by) % top, axis=1)


def load_shares(number_of, total, reach, skew, full):
    portions = [(1 << 20) // math.isqrt(standing ** skew) + 1 for standing in range(1, number_of + 1)]
    largest = reach if full else min(reach, max(-(-total // number_of), total * portions[0] // sum(portions)))
    least = 1 if total - largest >= number_of - 1 else 0
    holding, spare = [largest] + [least] * (number_of - 1), total - largest - least * (number_of - 1)
    while spare > 0:
        free = [i for i in range(1, number_of) if holding[i] < largest] or [i for i in range(1, number_of) if holding[i] < reach]
        whole, budget = sum([portions[i] for i in free]), spare
        for i in free:
            addition = min(reach - holding[i], max(1, budget * portions[i] // whole), spare)
            holding[i] = holding[i] + addition
            spare = spare - addition
    return np.array(holding)


def bell_draw(key, dims, deviation, limit, pieces=(), held_as=jnp.bfloat16):
    values = deviation * jax.random.normal(key, dims, jnp.float32)
    if pieces:
        values = values * level_of(key, dims, pieces, -0.22, 0.18)
    return jnp.clip(values, -limit, limit).astype(held_as)


def setup_inputs(seed: int = 0) -> dict:
    seeds = jax.random.split(jax.random.key(seed), 10)
    saved_pre = bell_draw(seeds[0], (ROWS, TOP, 2 * FF), 1.0, 6.0, ((0, 256),))
    layer_grad = bell_draw(seeds[1], (ROWS, D), 0.25, 4.0, ((0, 256),))
    router_weight = jnp.clip(jnp.exp(math.log(0.5) - 2.306499 * jax.random.uniform(seeds[2], (ROWS, TOP), jnp.float32) ** level_of(seeds[2], (ROWS, TOP), ((0, 256),), -0.2, 0.2)), 0.049804688, 0.5).astype(jnp.bfloat16)
    routes_keys = jax.random.split(jax.random.fold_in(seeds[3], 1), ROWS // TOK_DEV)
    routes_turns = jax.random.permutation(jax.random.fold_in(seeds[3], 3), ROWS // TOK_DEV)
    routes = jax.vmap(lambda own, number: deal_out(jax.random.fold_in(seeds[3], 2), own, number, TOK_DEV, EXPERTS, TOP, CAP, 2))(routes_keys, routes_turns).reshape((ROWS, TOP))
    queries = bell_draw(seeds[4], (DATA_GROUPS, SEQUENCE_TOKENS, HEADS * HEAD_K), (4 * SEQUENCE_TOKENS ** -0.5), 0.625, ((0, 4), (1, 64)))
    key_vectors = bell_draw(seeds[5], (DATA_GROUPS, SEQUENCE_TOKENS, HEADS * HEAD_K), (HEAD_K ** -0.5), 2.0, ((0, 4), (1, 64)))
    value_vectors = bell_draw(seeds[6], (DATA_GROUPS, SEQUENCE_TOKENS, HEADS * HEAD_K), (HEAD_K ** -0.5), 2.0, ((0, 4), (1, 64)))
    head_grad = bell_draw(seeds[7], (DATA_GROUPS, SEQUENCE_TOKENS, HEADS * HEAD_K), 1.0, 6.0, ((0, 4), (1, 64)))
    log_gate = draw_log_gate(jax.random.fold_in(seeds[9], 71), 0)
    return {"saved_pre": saved_pre, "layer_grad": layer_grad, "router_weight": router_weight, "routes": routes, "queries": queries, "key_vectors": key_vectors, "value_vectors": value_vectors, "head_grad": head_grad, "log_gate": log_gate}


def head_backward(query_rows, key_rows, value_rows, grad_rows, gate_rows):
    shape = (SEQUENCE_TOKENS, HEADS, HEAD_K)
    query_f = query_rows.astype(jnp.float32).reshape(shape)
    key_f = key_rows.astype(jnp.float32).reshape(shape)
    value_float = value_rows.astype(jnp.float32).reshape(shape)
    gradient_float = grad_rows.astype(jnp.float32).reshape(shape)
    decay = jnp.exp(gate_rows.reshape(shape))

    def step(carry, inputs):
        query_t, grad_t, key_t, value_t, decay_t = inputs
        state_grad = query_t[:, :, None] * grad_t[:, None, :] + carry
        key_out = jnp.sum(state_grad * value_t[:, None, :], axis=2)
        value_out = jnp.sum(state_grad * key_t[:, :, None], axis=1)
        return decay_t[:, :, None] * state_grad, (key_out, value_out)

    start = jnp.zeros((HEADS, HEAD_K, HEAD_K), jnp.float32)
    _, outs = lax.scan(step, start, (query_f, gradient_float, key_f, value_float, decay), reverse=True)
    key_out = outs[0].reshape(SEQUENCE_TOKENS, HEADS * HEAD_K).astype(jnp.bfloat16)
    value_out = outs[1].reshape(SEQUENCE_TOKENS, HEADS * HEAD_K).astype(jnp.bfloat16)
    return key_out, value_out


def reference(saved_pre, layer_grad, router_weight, routes, queries, key_vectors, value_vectors, head_grad, log_gate):
    key_list = []
    value_list = []
    for group in range(DATA_GROUPS):
        key_out, value_out = head_backward(queries[group], key_vectors[group], value_vectors[group], head_grad[group], log_gate[group])
        key_list.append(key_out)
        value_list.append(value_out)
    key_grad = jnp.stack(key_list)
    value_grad = jnp.stack(value_list)

    total_rows = layer_grad.shape[0]
    most_rows = CAP * (total_rows // TOK_DEV)
    flat_ids = routes.reshape(-1)
    flat_weight = jnp.concatenate([router_weight.reshape(-1).astype(jnp.float32), jnp.zeros((1,), jnp.float32)])
    flat_pre = jnp.concatenate([saved_pre.reshape(-1, 2 * FF), jnp.zeros((1, 2 * FF), saved_pre.dtype)])
    padded_grad = jnp.concatenate([layer_grad, jnp.zeros((1, layer_grad.shape[1]), layer_grad.dtype)])

    def one_expert(expert):
        where = jnp.nonzero(flat_ids == expert, size=most_rows, fill_value=flat_ids.shape[0])[0].astype(jnp.int32)
        source = (where // TOP).astype(jnp.int32)
        pair_grad = (padded_grad[source].astype(jnp.float32) * flat_weight[where][:, None]).astype(jnp.bfloat16)
        pre_rows = flat_pre[where].astype(jnp.float32)
        pair_hidden = (jax.nn.silu(pre_rows[:, :FF]) * pre_rows[:, FF:]).astype(jnp.bfloat16)
        return jnp.dot(pair_hidden.T, pair_grad, preferred_element_type=jnp.float32).astype(jnp.bfloat16)

    down_grad = lax.map(one_expert, jnp.arange(EXPERTS, dtype=jnp.int32))
    return key_grad, value_grad, down_grad
```

```python
import functools

import jax
import jax.numpy as jnp
from jax import lax
from jax.experimental import pallas as pl
from jax.experimental.pallas import tpu as pltpu
from jax.sharding import PartitionSpec as P

FF = 512
TOK = 128
D = 2304
Z = 8
W = 8
DP = 4
CAP = 9
TOP = 8
PAIRS = TOK * TOP
PIECES = 6
PC = D // PIECES
UNIT = D // 12
OWN = D // DP
LANES = 128
MESH = pl.DeviceIdType.MESH
F32 = jnp.float32
BF16 = jnp.bfloat16


def iota(shape, dim):
    return lax.broadcasted_iota(jnp.int32, shape, dim)


def dot(a, b):
    return lax.dot_general(a, b, (((1,), (0,)), ((), ())), preferred_element_type=F32)


def dot_nt(a, b):
    return lax.dot_general(a, b, (((1,), (1,)), ((), ())), preferred_element_type=F32)


def dot_tn(a, b):
    return lax.dot_general(a, b, (((0,), (0,)), ((), ())), preferred_element_type=F32)


def split2(x):
    hi = x.astype(BF16)
    return hi, (x - hi.astype(F32)).astype(BF16)


def kernel(
    pre_ref, g_ref, rt_ref, wt_ref, q_ref, k_ref, v_ref, do_ref, lg_ref,
    kg_ref, vg_ref, dg_ref,
    ga, hid, sh, hin, pa, hy, hr, hm, yb, rx, xt, su, rs, acc,
    cum, a_s, a_r, b_s, b_r, cl, c_s, c_r,
    ag_ss, ag_rs, hz_ss, hz_rs, hw_ss, hw_rs, y_ss, y_rs, rs_ss, rs_rs,
    a_ss, a_rs, b_ss, b_rs, c_ss, c_rs,
):
    dp = lax.axis_index("dp")
    ctx = lax.axis_index("ctx")
    z = ctx // W
    w = ctx % W

    def z_peer(t):
        return {"ctx": t * W + w}

    def w_peer(t):
        return {"ctx": z * W + t}

    def remote(src, dst, ss, rsem, dev):
        return pltpu.make_async_remote_copy(
            src_ref=src, dst_ref=dst, send_sem=ss, recv_sem=rsem, device_id=dev, device_id_type=MESH
        )

    barrier = pltpu.get_barrier_semaphore()
    for o in range(1, Z):
        pl.semaphore_signal(barrier, inc=1, device_id=z_peer((z + o) % Z), device_id_type=MESH)
        pl.semaphore_signal(barrier, inc=1, device_id=w_peer((w + o) % W), device_id_type=MESH)
    for o in range(1, DP):
        pl.semaphore_signal(barrier, inc=1, device_id={"dp": (dp + o) % DP}, device_id_type=MESH)
    pl.semaphore_wait(barrier, (Z - 1) + (W - 1) + (DP - 1))

    first_piece = (2 + (3 * dp) // 2) % PIECES

    def piece_of(i):
        return (first_piece + i) % PIECES

    def hops(i, way):
        return 4 if (i % 2 == 0) == (way == 0) else 3

    def ag_copy(i, way, step):
        src = (z - step + Z) % Z if way == 0 else (z + step) % Z
        to = (z + 1) % Z if way == 0 else (z + Z - 1) % Z
        return remote(ga.at[i, src], ga.at[i, src], ag_ss.at[i, way, step], ag_rs.at[i, way, step], z_peer(to))

    def ag_arrival(i, way, step):
        src = (z - 1 - step + 2 * Z) % Z if way == 0 else (z + 1 + step) % Z
        return remote(
            ga.at[i, src], ga.at[i, src], ag_ss.at[i, way, step], ag_rs.at[i, way, step], z_peer((z + 1) % Z)
        )

    for i in range(PIECES):
        ga[i, z] = g_ref[:, pl.ds(pl.multiple_of(piece_of(i) * PC, LANES), PC)]
        ag_copy(i, 0, 0).start()
        ag_copy(i, 1, 0).start()

    def forward(i, step):
        for way in range(2):
            if step < hops(i, way):
                ag_arrival(i, way, step - 1).wait_recv()
                ag_copy(i, way, step).start()

    def hidden_block(n, carry):
        x = pre_ref[pl.ds(n * 16, 16)].astype(F32).reshape(LANES, 2 * FF)
        gate, up = x[:, :FF], x[:, FF:]
        hid[pl.ds(pl.multiple_of(n * LANES, LANES), LANES), :] = (gate / (1.0 + jnp.exp(-gate)) * up).astype(BF16)
        return carry

    lax.fori_loop(0, PAIRS // LANES, hidden_block, 0)

    named = iota((LANES, PAIRS), 0) == rt_ref[...]
    named_f = jnp.where(named, 1.0, 0.0)
    token_of = jnp.where(iota((PAIRS, TOK), 0) // TOP == iota((PAIRS, TOK), 1), 1.0, 0.0).astype(BF16)
    by_token = dot(named_f.astype(BF16), token_of)
    weight = dot(jnp.where(named, wt_ref[...], 0.0).astype(BF16), token_of)
    before = jnp.where(iota((TOK, TOK), 0) < iota((TOK, TOK), 1), 1.0, 0.0).astype(BF16)
    rank = dot(by_token.astype(BF16), before)
    rank_pair = dot_nt(rank.astype(BF16), token_of)
    rank_pair = jnp.where(named, rank_pair, -1.0)
    rank = jnp.where(by_token > 0.5, rank, -1.0)
    for r in range(CAP):
        pa[r] = jnp.where(rank_pair == float(r), 1.0, 0.0).astype(BF16)
        sh[r, :, FF:] = jnp.where(rank == float(r), weight, 0.0).astype(BF16)

    def sort_block(n, carry):
        pick = pa[pl.ds(3 * n, 3)].reshape(3 * LANES, PAIRS)
        sh[pl.ds(3 * n, 3), :, :FF] = dot(pick, hid[...]).astype(BF16).reshape(3, LANES, FF)
        return carry

    lax.fori_loop(0, 3, sort_block, 0)

    def hz_copy(t):
        return remote(sh.at[:, pl.ds(pl.multiple_of(16 * t, 16), 16)], hin.at[:, z], hz_ss.at[t], hz_rs.at[z], z_peer(t))

    def hz_arrival(s):
        return remote(hin.at[:, z], hin.at[:, s], hz_ss.at[s], hz_rs.at[s], z_peer(s))

    for o in (4, 3, 5, 2, 6, 1, 7):
        hz_copy((z + o) % Z).start()
    hin[:, z] = sh[:, pl.ds(pl.multiple_of(16 * z, 16), 16)]

    lane = iota((LANES, LANES), 1)
    low = lane < 64
    low64 = iota((64, LANES), 1) < 64
    tri = jnp.where(iota((TOK, TOK), 1) <= iota((TOK, TOK), 0), 1.0, 0.0).astype(BF16)

    def attend_first(j, carry):
        at = pl.ds(pl.multiple_of(j * LANES, LANES), LANES)
        x = lg_ref[:, at]
        hi, rest = split2(x)
        mid, lo = split2(x - hi.astype(F32))
        total = dot(tri, hi) + (dot(tri, mid) + dot(tri, lo))
        cum[:, at] = total
        qh, ql = split2(q_ref[:, at].astype(F32) * jnp.exp(total))
        do = do_ref[:, at]
        s = dot_tn(qh, do) + dot_tn(ql, do)
        last = jnp.broadcast_to(total.T[:, TOK - 1 :], (LANES, LANES))
        a_s[j, :64] = jnp.where(low64, s[:64], s[64:])
        a_s[j, 64:] = jnp.where(low64, last[:64], last[64:])
        return carry

    lax.fori_loop(0, W, attend_first, 0)

    def a_copy(t):
        return remote(a_s.at[t], a_r.at[w], a_ss.at[t], a_rs.at[w], w_peer(t))

    def a_arrival(s):
        return remote(a_s.at[s], a_r.at[s], a_ss.at[s], a_rs.at[s], w_peer(s))

    for o in range(1, W):
        a_copy((w + o) % W).start()
    a_r[w] = a_s[w]

    def b_copy(t):
        return remote(b_s, b_r.at[z], b_ss.at[t], b_rs.at[z], z_peer(t))

    def b_arrival(s):
        return remote(b_s, b_r.at[s], b_ss.at[s], b_rs.at[s], z_peer(s))

    def attend_plane():
        for o in range(1, W):
            a_arrival((w + o) % W).wait_recv()
        c = jnp.zeros((64, LANES), F32)
        d = jnp.zeros((64, LANES), F32)
        for b in range(W - 1, -1, -1):
            cl[b, :64] = c
            cl[b, 64:] = d
            ld = a_r[b, 64:]
            c = a_r[b, :64] + jnp.exp(ld) * c
            d = d + ld
        b_s[:64] = c
        b_s[64:] = d
        for t in range(Z - 1):
            @pl.when(t < z)
            def _():
                b_copy(t).start()

    def c_copy(t):
        return remote(c_s.at[t], c_r.at[w], c_ss.at[t], c_rs.at[w], w_peer(t))

    def c_arrival(s):
        return remote(c_s.at[s], c_r.at[s], c_ss.at[s], c_rs.at[s], w_peer(s))

    def attend_carry():
        acc[:64, :LANES] = jnp.zeros((64, LANES), F32)
        for s in range(Z - 1, 0, -1):
            @pl.when(s > z)
            def _():
                b_arrival(s).wait_recv()
                acc[:64, :LANES] = b_r[s, :64] + jnp.exp(b_r[s, 64:]) * acc[:64, :LANES]
        x = acc[:64, :LANES]
        for b in range(W):
            c_s[b] = cl[b, :64] + jnp.exp(cl[b, 64:]) * x
        for o in range(1, W):
            c_copy((w + o) % W).start()
        c_r[w] = c_s[w]

    def attend_last():
        for o in range(1, W):
            c_arrival((w + o) % W).wait_recv()
        later = iota((TOK, TOK), 0) <= iota((TOK, TOK), 1)

        def pair(j, carry):
            at = pl.ds(pl.multiple_of(j * LANES, LANES), LANES)
            total = cum[:, at]
            middle = total[63:64]
            ek = jnp.exp(middle - total)
            tail = jnp.exp(total[TOK - 1 :] - total)
            k = k_ref[:, at].astype(F32)
            v = v_ref[:, at]
            do = do_ref[:, at]
            qs = q_ref[:, at].astype(F32) * jnp.exp(total - middle)
            ks = k * ek
            qh, ql = split2(qs)
            vo = jnp.zeros((TOK, LANES), F32)
            ko = jnp.zeros((TOK, LANES), F32)
            for half in (low, jnp.logical_not(low)):
                kh, kl = split2(jnp.where(half, ks, 0.0))
                scores = dot_nt(kh, qh) + (dot_nt(kh, ql) + dot_nt(kl, qh))
                sh_, sl_ = split2(jnp.where(later, scores, 0.0))
                dom = jnp.where(half, do.astype(F32), 0.0).astype(BF16)
                vo = vo + (dot(sh_, dom) + dot(sl_, dom))
                vm = jnp.where(half, v.astype(F32), 0.0).astype(BF16)
                bh, bl = split2(jnp.where(later, dot_nt(vm, do), 0.0))
                qmh, qml = split2(jnp.where(half, qs, 0.0))
                ko = ko + (dot(bh, qmh) + (dot(bl, qmh) + dot(bh, qml)))
            c = c_r[j]
            ch, clo = split2(jnp.concatenate([jnp.where(low64, c, 0.0), jnp.where(low64, 0.0, c)], axis=0))
            th, tl = split2(k * tail)
            vo = vo + (dot(th, ch) + (dot(th, clo) + dot(tl, ch)))
            ko = ek * ko + tail * (dot_nt(v, ch) + dot_nt(v, clo))
            kg_ref[:, at] = ko.astype(BF16)
            vg_ref[:, at] = vo.astype(BF16)
            return carry

        lax.fori_loop(0, W, pair, 0)

    def hw_copy(t):
        return remote(
            hy.at[:, pl.ds(pl.multiple_of(16 * t, 16), 16)], hr.at[pl.ds(CAP * w, CAP)], hw_ss.at[t], hw_rs.at[w], w_peer(t)
        )

    def hw_arrival(s):
        return remote(hr.at[pl.ds(CAP * s, CAP)], hr.at[pl.ds(CAP * s, CAP)], hw_ss.at[s], hw_rs.at[s], w_peer(s))

    def hidden_plane():
        for o in range(1, Z):
            hz_arrival((z + o) % Z).wait_recv()
        row = iota((LANES, LANES), 0)
        col = iota((LANES, LANES), 1)
        same = (row // 2) % 8 == col // 16
        place = jnp.where(same & (col % 16 == 2 * (row // 16) + row % 2), 1.0, 0.0).astype(BF16)
        source = (row // 2) % 8

        def one(r, carry):
            x = dot(place, hin[r].reshape(LANES, FF + LANES))
            hy[r] = x[:, :FF].astype(BF16)
            p = x[:, FF:]
            for s in range(Z):
                pa[r, :, s * LANES : (s + 1) * LANES] = jnp.where(source == s, p, 0.0).astype(BF16)
            return carry

        lax.fori_loop(0, CAP, one, 0)
        for o in range(1, W):
            hw_copy((w + o) % W).start()
        hr[pl.ds(CAP * w, CAP)] = hy[:, pl.ds(pl.multiple_of(16 * w, 16), 16)]

    def hidden_wide():
        for o in range(1, W):
            hw_arrival((w + o) % W).wait_recv()

        def one(m, carry):
            x = hr[pl.ds(8 * m, 8)].reshape(LANES, FF).astype(F32)
            first = iota((LANES, FF), 0) % 2 == 0
            at = pl.ds(pl.multiple_of(m * LANES, LANES), LANES)
            hm[at, :FF] = jnp.where(first, x, 0.0).astype(BF16)
            hm[at, FF:] = jnp.where(first, 0.0, x).astype(BF16)
            return carry

        lax.fori_loop(0, CAP, one, 0)

    def y_copy(i, t):
        return remote(
            yb.at[i, :, pl.ds(pl.multiple_of(16 * t, 16), 16)],
            rx.at[i, pl.ds(CAP * w, CAP)],
            y_ss.at[i, t],
            y_rs.at[i, w],
            w_peer(t),
        )

    def y_arrival(i, s):
        at = pl.ds(CAP * s, CAP)
        return remote(rx.at[i, at], rx.at[i, at], y_ss.at[i, s], y_rs.at[i, s], w_peer(s))

    def gather_piece(i):
        for way in range(2):
            ag_arrival(i, way, hops(i, way) - 1).wait_recv()

        def one(n, carry):
            pick = pa[pl.ds(3 * n, 3)].reshape(3 * LANES, Z * TOK)
            yb[i, pl.ds(3 * n, 3)] = dot(pick, ga[i].reshape(Z * TOK, PC)).astype(BF16).reshape(3, LANES, PC)
            return carry

        lax.fori_loop(0, 3, one, 0)
        for o in range(1, W):
            y_copy(i, (w + o) % W).start()
        rx[i, pl.ds(CAP * w, CAP)] = yb[i, :, pl.ds(pl.multiple_of(16 * w, 16), 16)]

    def unit_of(i, j):
        u = 2 * piece_of(i) + j
        return u // 3, u % 3

    def rs_copy(i, j):
        owner, at = unit_of(i, j)
        return remote(su.at[2 * i + j], rs.at[at, dp], rs_ss.at[2 * i + j], rs_rs.at[at, dp], {"dp": owner})

    def rs_arrival(at, s):
        return remote(su.at[0], rs.at[at, s], rs_ss.at[0], rs_rs.at[at, s], {"dp": s})

    def product_piece(i):
        for o in range(1, W):
            y_arrival(i, (w + o) % W).wait_recv()
        for m in range(CAP):
            xt[:, m * LANES : (m + 1) * LANES] = rx[i, 8 * m : 8 * m + 8].reshape(LANES, PC).T

        def one(n, carry):
            at = pl.ds(pl.multiple_of(n * 256, 256), 256)
            out = dot(xt[...], hm[:, at]).astype(BF16)
            su[2 * i, :, at] = out[:UNIT]
            su[2 * i + 1, :, at] = out[UNIT:]
            return carry

        lax.fori_loop(0, 4, one, 0)
        for j in range(2):
            owner, at = unit_of(i, j)

            @pl.when(owner != dp)
            def _():
                rs_copy(i, j).start()

            @pl.when(owner == dp)
            def _():
                rs[at, dp] = su[2 * i + j]

    attend_plane()
    for i in range(PIECES):
        forward(i, 1)
    attend_carry()
    for i in range(2):
        forward(i, 2)
    hidden_plane()
    for slot in range(PIECES + 2):
        if slot + 2 < PIECES:
            forward(slot + 2, 2)
        if slot < PIECES:
            forward(slot, 3)
        if 0 <= slot - 1 < PIECES:
            gather_piece(slot - 1)
        if slot == 1:
            attend_last()
        if slot == 2:
            hidden_wide()
        if 0 <= slot - 2 < PIECES:
            product_piece(slot - 2)

    for o in range(1, DP):
        for at in range(3):
            rs_arrival(at, (dp + o) % DP).wait_recv()
    for at in range(3):
        acc[at * UNIT : (at + 1) * UNIT] = (
            (rs[at, 0].astype(F32) + rs[at, 1].astype(F32)) + (rs[at, 2].astype(F32) + rs[at, 3].astype(F32))
        )

    def turn(n, carry):
        at = pl.ds(pl.multiple_of(n * LANES, LANES), LANES)
        dg_ref[at, :] = acc[:, at].T.astype(BF16)
        return carry

    lax.fori_loop(0, 8, turn, 0)

    for i in range(PIECES):
        for way in range(2):
            for step in range(hops(i, way)):
                ag_copy(i, way, step).wait_send()
        for o in range(1, W):
            y_copy(i, (w + o) % W).wait_send()
        for j in range(2):
            @pl.when(unit_of(i, j)[0] != dp)
            def _():
                rs_copy(i, j).wait_send()
    for o in range(1, Z):
        hz_copy((z + o) % Z).wait_send()
        hw_copy((w + o) % W).wait_send()
        a_copy((w + o) % W).wait_send()
        c_copy((w + o) % W).wait_send()
    for t in range(Z - 1):
        @pl.when(t < z)
        def _():
            b_copy(t).wait_send()


def on_device(saved_pre, layer_grad, router_weight, routes, queries, key_vectors, value_vectors, head_grad, log_gate):
    vmem = pl.BlockSpec(memory_space=pltpu.VMEM)
    dma = pltpu.SemaphoreType.DMA
    key_grad, value_grad, down_grad = pl.pallas_call(
        kernel,
        out_shape=(
            jax.ShapeDtypeStruct((TOK, 1024), BF16),
            jax.ShapeDtypeStruct((TOK, 1024), BF16),
            jax.ShapeDtypeStruct((1024, OWN), BF16),
        ),
        in_specs=[vmem] * 9,
        out_specs=(vmem, vmem, vmem),
        scratch_shapes=[
            pltpu.VMEM((PIECES, Z, TOK, PC), BF16),
            pltpu.VMEM((PAIRS, FF), BF16),
            pltpu.VMEM((CAP, LANES, FF + LANES), BF16),
            pltpu.VMEM((CAP, Z, 16, FF + LANES), BF16),
            pltpu.VMEM((CAP, LANES, Z * TOK), BF16),
            pltpu.VMEM((CAP, LANES, FF), BF16),
            pltpu.VMEM((W * CAP, 16, FF), BF16),
            pltpu.VMEM((W * CAP * 16, 2 * FF), BF16),
            pltpu.VMEM((PIECES, CAP, LANES, PC), BF16),
            pltpu.VMEM((PIECES, W * CAP, 16, PC), BF16),
            pltpu.VMEM((PC, W * CAP * 16), BF16),
            pltpu.VMEM((12, UNIT, 2 * FF), BF16),
            pltpu.VMEM((3, DP, UNIT, 2 * FF), BF16),
            pltpu.VMEM((OWN, 2 * FF), F32),
            pltpu.VMEM((TOK, 1024), F32),
            pltpu.VMEM((W, LANES, LANES), F32),
            pltpu.VMEM((W, LANES, LANES), F32),
            pltpu.VMEM((LANES, LANES), F32),
            pltpu.VMEM((Z, LANES, LANES), F32),
            pltpu.VMEM((W, LANES, LANES), F32),
            pltpu.VMEM((W, 64, LANES), F32),
            pltpu.VMEM((W, 64, LANES), F32),
            dma((PIECES, 2, 4)),
            dma((PIECES, 2, 4)),
            dma((Z,)),
            dma((Z,)),
            dma((W,)),
            dma((W,)),
            dma((PIECES, W)),
            dma((PIECES, W)),
            dma((12,)),
            dma((3, DP)),
            dma((W,)),
            dma((W,)),
            dma((Z,)),
            dma((Z,)),
            dma((W,)),
            dma((W,)),
        ],
        compiler_params=pltpu.CompilerParams(
            collective_id=0, has_side_effects=True, vmem_limit_bytes=60 * 1024 * 1024
        ),
        cost_estimate=pl.CostEstimate(flops=16_000_000_000, bytes_accessed=8_000_000, transcendentals=1_000_000),
    )(
        saved_pre,
        layer_grad,
        routes.reshape(1, PAIRS),
        router_weight.reshape(1, PAIRS).astype(F32),
        queries[0],
        key_vectors[0],
        value_vectors[0],
        head_grad[0],
        log_gate[0],
    )
    return key_grad[None], value_grad[None], down_grad.reshape(2, FF, OWN)


def solution(mesh):
    return jax.shard_map(
        on_device,
        mesh=mesh,
        in_specs=(
            P(("dp", "ctx"), None, None),
            P(("dp", "ctx"), None),
            P(("dp", "ctx"), None),
            P(("dp", "ctx"), None),
            P("dp", "ctx", None),
            P("dp", "ctx", None),
            P("dp", "ctx", None),
            P("dp", "ctx", None),
            P("dp", "ctx", None),
        ),
        out_specs=(P("dp", "ctx", None), P("dp", "ctx", None), P("ctx", None, "dp")),
        check_vma=False,
    )
```

```python
import functools

import jax
import jax.numpy as jnp
from jax import lax
from jax.experimental import pallas as pl
from jax.experimental.pallas import tpu as pltpu
from jax.sharding import PartitionSpec as P

FF = 512
HALF = FF // 2
TOK = 128
D = 2304
Z = 8
W = 8
DP = 4
CAP = 9
TOP = 8
PAIRS = TOK * TOP
PIECES = 6
PC = D // PIECES
UNIT = D // 12
OWN = D // DP
LANES = 128
MESH = pl.DeviceIdType.MESH
F32 = jnp.float32
BF16 = jnp.bfloat16


def iota(shape, dim):
    return lax.broadcasted_iota(jnp.int32, shape, dim)


def dot(a, b):
    return lax.dot_general(a, b, (((1,), (0,)), ((), ())), preferred_element_type=F32)


def dot_nt(a, b):
    return lax.dot_general(a, b, (((1,), (1,)), ((), ())), preferred_element_type=F32)


def dot_tn(a, b):
    return lax.dot_general(a, b, (((0,), (0,)), ((), ())), preferred_element_type=F32)


def split2(x):
    hi = x.astype(BF16)
    return hi, (x - hi.astype(F32)).astype(BF16)


def kernel(
    pre_ref, g_ref, rt_ref, wt_ref, q_ref, k_ref, v_ref, do_ref, lg_ref,
    kg_ref, vg_ref, dg_ref,
    ga, hid, sh, hin, pa, hy, hr, hm, yb, rx, xt, su, rs, acc,
    cum, tb_s, tb_r, pt, a_s, a_r, b_s, b_r, cl, c_s, c_r,
    ag_ss, ag_rs, t_ss, t_rs, hz_ss, hz_rs, hw_ss, hw_rs, y_ss, y_rs, rs_ss, rs_rs,
    a_ss, a_rs, b_ss, b_rs, c_ss, c_rs,
):
    dp = lax.axis_index("dp")
    ctx = lax.axis_index("ctx")
    z = ctx // W
    w = ctx % W

    def z_peer(t):
        return {"ctx": t * W + w}

    def w_peer(t):
        return {"ctx": z * W + t}

    def remote(src, dst, ss, rsem, dev):
        return pltpu.make_async_remote_copy(
            src_ref=src, dst_ref=dst, send_sem=ss, recv_sem=rsem, device_id=dev, device_id_type=MESH
        )

    barrier = pltpu.get_barrier_semaphore()
    for o in range(1, Z):
        pl.semaphore_signal(barrier, inc=1, device_id=z_peer((z + o) % Z), device_id_type=MESH)
        pl.semaphore_signal(barrier, inc=1, device_id=w_peer((w + o) % W), device_id_type=MESH)
    for o in range(1, DP):
        pl.semaphore_signal(barrier, inc=1, device_id={"dp": (dp + o) % DP}, device_id_type=MESH)

    def all_here():
        pl.semaphore_wait(barrier, (Z - 1) + (W - 1) + (DP - 1))

    first_piece = (2 + (3 * dp) // 2) % PIECES

    def piece_of(i):
        return (first_piece + i) % PIECES

    def hops(i, way):
        return 4 if (i % 2 == 0) == (way == 0) else 3

    def ag_copy(i, way, step):
        src = (z - step + Z) % Z if way == 0 else (z + step) % Z
        to = (z + 1) % Z if way == 0 else (z + Z - 1) % Z
        return remote(ga.at[i, src], ga.at[i, src], ag_ss.at[i, way, step], ag_rs.at[i, way, step], z_peer(to))

    def ag_arrival(i, way, step):
        src = (z - 1 - step + 2 * Z) % Z if way == 0 else (z + 1 + step) % Z
        return remote(
            ga.at[i, src], ga.at[i, src], ag_ss.at[i, way, step], ag_rs.at[i, way, step], z_peer((z + 1) % Z)
        )

    def start_piece(i):
        ga[i, z] = g_ref[:, pl.ds(pl.multiple_of(piece_of(i) * PC, LANES), PC)]
        ag_copy(i, 0, 0).start()
        ag_copy(i, 1, 0).start()

    def forward(i, step):
        for way in range(2):
            if step < hops(i, way):
                ag_arrival(i, way, step - 1).wait_recv()
                ag_copy(i, way, step).start()

    def t_copy(t):
        return remote(tb_s, tb_r.at[z], t_ss.at[t], t_rs.at[z], z_peer(t))

    def t_arrival(s):
        return remote(tb_s, tb_r.at[s], t_ss.at[s], t_rs.at[s], z_peer(s))

    def make_tables():
        tb_s[:TOP] = rt_ref[...].astype(F32)
        tb_s[TOP:] = wt_ref[...].astype(F32)

    def send_tables():
        for o in range(1, Z):
            t_copy((z + o) % Z).start()
        tb_r[z] = tb_s[...]

    before = jnp.where(iota((TOK, TOK), 0) < iota((TOK, TOK), 1), 1.0, 0.0).astype(BF16)

    def hidden_first():
        def hidden_block(n, carry):
            x = pre_ref[pl.ds(n * 16, 16)].astype(F32).reshape(LANES, 2 * FF)
            gate, up = x[:, :FF], x[:, FF:]
            hid[pl.ds(pl.multiple_of(n * LANES, LANES), LANES), :] = (gate / (1.0 + jnp.exp(-gate)) * up).astype(BF16)
            return carry

        lax.fori_loop(0, PAIRS // LANES, hidden_block, 0)

    def expert_at(shape):
        row = iota(shape, 0)
        return (row // 2) % 8 * 16 + row // 16 * 2 + row % 2

    def hidden_sort():
        expert = expert_at((LANES, TOK)).astype(F32)
        by_token = jnp.zeros((LANES, TOK), F32)
        for j in range(TOP):
            by_token = by_token + jnp.where(tb_s[j : j + 1] == expert, 1.0, 0.0)
        rank = dot(by_token.astype(BF16), before)
        rank = jnp.where(by_token > 0.5, rank, -1.0)
        token_of = jnp.where(iota((PAIRS, TOK), 0) // TOP == iota((PAIRS, TOK), 1), 1.0, 0.0).astype(BF16)
        wide = dot_nt(tb_s[:TOP].astype(BF16), token_of)
        chosen = iota((TOP, PAIRS), 0) == iota((TOP, PAIRS), 1) % TOP
        route = jnp.sum(jnp.where(chosen, wide, 0.0), axis=0, keepdims=True)
        rank_pair = jnp.where(route == expert_at((LANES, PAIRS)).astype(F32), dot_nt(rank.astype(BF16), token_of), -1.0)
        for r in range(CAP):
            pa[r] = jnp.where(rank_pair == float(r), 1.0, 0.0).astype(BF16)

        def sort_block(n, carry):
            pick = pa[pl.ds(3 * n, 3)].reshape(3 * LANES, PAIRS)
            x = dot(pick, hid[...]).astype(BF16)
            sh[0, pl.ds(3 * n, 3)] = x[:, :HALF].reshape(3, LANES, HALF)
            sh[1, pl.ds(3 * n, 3)] = x[:, HALF:].reshape(3, LANES, HALF)
            return carry

        lax.fori_loop(0, 3, sort_block, 0)

    def hw_copy(h, t):
        at = pl.ds(pl.multiple_of(16 * t, 16), 16)
        return remote(sh.at[h, :, at], hin.at[h, :, w], hw_ss.at[h, t], hw_rs.at[h, w], w_peer(t))

    def hw_arrival(h, s):
        return remote(hin.at[h, :, w], hin.at[h, :, s], hw_ss.at[h, s], hw_rs.at[h, s], w_peer(s))

    def hidden_send(h):
        for o in range(1, W):
            hw_copy(h, (w + o) % W).start()
        hin[h, :, w] = sh[h, :, pl.ds(pl.multiple_of(16 * w, 16), 16)]

    lane = iota((LANES, LANES), 1)
    low = lane < 64
    low64 = iota((64, LANES), 1) < 64
    tri = jnp.where(iota((TOK, TOK), 1) <= iota((TOK, TOK), 0), 1.0, 0.0).astype(BF16)

    def attend_first(j, carry):
        at = pl.ds(pl.multiple_of(j * LANES, LANES), LANES)
        x = lg_ref[:, at]
        hi, rest = split2(x)
        mid, lo = split2(x - hi.astype(F32))
        total = dot(tri, hi) + (dot(tri, mid) + dot(tri, lo))
        cum[:, at] = total
        qh, ql = split2(q_ref[:, at].astype(F32) * jnp.exp(total))
        do = do_ref[:, at]
        s = dot_tn(qh, do) + dot_tn(ql, do)
        a_s[j, :64] = jnp.where(low64, s[:64], s[64:])
        a_s[j, 64:] = jnp.broadcast_to(total[TOK - 1 :], (8, LANES))
        return carry

    def a_copy(t):
        return remote(a_s.at[t], a_r.at[w], a_ss.at[t], a_rs.at[w], w_peer(t))

    def a_arrival(s):
        return remote(a_s.at[s], a_r.at[s], a_ss.at[s], a_rs.at[s], w_peer(s))

    def attend_block():
        lax.fori_loop(0, W, attend_first, 0)

    def attend_send():
        for o in range(1, W):
            a_copy((w + o) % W).start()
        a_r[w] = a_s[w]

    def down_channels(row):
        x = jnp.broadcast_to(row, (LANES, LANES)).T
        return jnp.where(low64, x[:64], x[64:])

    def b_copy(t):
        return remote(b_s, b_r.at[z], b_ss.at[t], b_rs.at[z], z_peer(t))

    def b_arrival(s):
        return remote(b_s, b_r.at[s], b_ss.at[s], b_rs.at[s], z_peer(s))

    def attend_plane():
        for o in range(1, W):
            a_arrival((w + o) % W).wait_recv()
        c = jnp.zeros((64, LANES), F32)
        d = jnp.zeros((64, LANES), F32)
        whole = jnp.zeros((8, LANES), F32)
        for b in range(W - 1, -1, -1):
            cl[b, :64] = c
            cl[b, 64:] = d
            ld = down_channels(a_r[b, 64:65])
            c = a_r[b, :64] + jnp.exp(ld) * c
            d = d + ld
            whole = whole + a_r[b, 64:]
        b_s[:64] = c
        b_s[64:] = whole
        for t in range(Z - 1):
            @pl.when(t < z)
            def _():
                b_copy(t).start()

    def c_copy(t):
        return remote(c_s.at[t], c_r.at[w], c_ss.at[t], c_rs.at[w], w_peer(t))

    def c_arrival(s):
        return remote(c_s.at[s], c_r.at[s], c_ss.at[s], c_rs.at[s], w_peer(s))

    def attend_carry():
        acc[...] = jnp.zeros((64, LANES), F32)
        for s in range(Z - 1, 0, -1):
            @pl.when(s > z)
            def _():
                b_arrival(s).wait_recv()
                acc[...] = b_r[s, :64] + jnp.exp(down_channels(b_r[s, 64:65])) * acc[...]
        x = acc[...]
        for b in range(W):
            c_s[b] = cl[b, :64] + jnp.exp(cl[b, 64:]) * x
        for o in range(1, W):
            c_copy((w + o) % W).start()
        c_r[w] = c_s[w]

    def attend_last():
        for o in range(1, W):
            c_arrival((w + o) % W).wait_recv()
        later = iota((TOK, TOK), 0) <= iota((TOK, TOK), 1)

        def pair(j, carry):
            at = pl.ds(pl.multiple_of(j * LANES, LANES), LANES)
            total = cum[:, at]
            middle = total[63:64]
            ek = jnp.exp(middle - total)
            tail = jnp.exp(total[TOK - 1 :] - total)
            k = k_ref[:, at].astype(F32)
            v = v_ref[:, at]
            do = do_ref[:, at]
            qs = q_ref[:, at].astype(F32) * jnp.exp(total - middle)
            ks = k * ek
            qh, ql = split2(qs)
            vo = jnp.zeros((TOK, LANES), F32)
            ko = jnp.zeros((TOK, LANES), F32)
            for half in (low, jnp.logical_not(low)):
                kh, kl = split2(jnp.where(half, ks, 0.0))
                scores = dot_nt(kh, qh) + (dot_nt(kh, ql) + dot_nt(kl, qh))
                sh_, sl_ = split2(jnp.where(later, scores, 0.0))
                dom = jnp.where(half, do.astype(F32), 0.0).astype(BF16)
                vo = vo + (dot(sh_, dom) + dot(sl_, dom))
                vm = jnp.where(half, v.astype(F32), 0.0).astype(BF16)
                bh, bl = split2(jnp.where(later, dot_nt(vm, do), 0.0))
                qmh, qml = split2(jnp.where(half, qs, 0.0))
                ko = ko + (dot(bh, qmh) + (dot(bl, qmh) + dot(bh, qml)))
            c = c_r[j]
            ch, clo = split2(jnp.concatenate([jnp.where(low64, c, 0.0), jnp.where(low64, 0.0, c)], axis=0))
            th, tl = split2(k * tail)
            vo = vo + (dot(th, ch) + (dot(th, clo) + dot(tl, ch)))
            ko = ek * ko + tail * (dot_nt(v, ch) + dot_nt(v, clo))
            kg_ref[:, at] = ko.astype(BF16)
            vg_ref[:, at] = vo.astype(BF16)
            return carry

        lax.fori_loop(0, W, pair, 0)

    def hz_copy(h, t):
        at = pl.ds(pl.multiple_of(16 * t, 16), 16)
        return remote(hy.at[h, :, at], hr.at[h, :, z], hz_ss.at[h, t], hz_rs.at[h, z], z_peer(t))

    def hz_arrival(h, s):
        return remote(hr.at[h, :, z], hr.at[h, :, s], hz_ss.at[h, s], hz_rs.at[h, s], z_peer(s))

    def placing():
        row = iota((LANES, LANES), 0)
        col = iota((LANES, LANES), 1)
        same = (row // 2) % 8 == col // 16
        return jnp.where(same & (col % 16 == 2 * (row // 16) + row % 2), 1.0, 0.0).astype(BF16)

    def weights_plane():
        for o in range(1, Z):
            t_arrival((z + o) % Z).wait_recv()
        expert = (iota((16, TOK), 0) + 16 * z).astype(F32)
        for s in range(Z):
            count = jnp.zeros((16, TOK), F32)
            weight = jnp.zeros((16, TOK), F32)
            for j in range(TOP):
                hit = tb_r[s, j : j + 1] == expert
                count = count + jnp.where(hit, 1.0, 0.0)
                weight = weight + jnp.where(hit, tb_r[s, TOP + j : TOP + j + 1], 0.0)
            pt[16 * s : 16 * s + 16] = count
            pt[LANES + 16 * s : LANES + 16 * s + 16] = weight
        count = pt[:LANES]
        rank = jnp.where(count > 0.5, dot(count.astype(BF16), before), -1.0)
        rank = dot(placing(), rank.astype(BF16))
        weight = dot(placing(), pt[LANES:].astype(BF16))
        source = (iota((LANES, TOK), 0) // 2) % Z
        for r in range(CAP):
            mine = jnp.where(rank == float(r), weight, 0.0)
            for s in range(Z):
                pa[r, :, s * LANES : (s + 1) * LANES] = jnp.where(source == s, mine, 0.0).astype(BF16)

    def hidden_plane(h):
        for o in range(1, W):
            hw_arrival(h, (w + o) % W).wait_recv()

        def one(r, carry):
            hy[h, r] = dot(placing(), hin[h, r].reshape(LANES, HALF)).astype(BF16)
            return carry

        lax.fori_loop(0, CAP, one, 0)
        for o in (4, 3, 5, 2, 6, 1, 7):
            hz_copy(h, (z + o) % Z).start()
        hr[h, :, z] = hy[h, :, pl.ds(pl.multiple_of(16 * z, 16), 16)]

    def hidden_wide(h):
        for o in range(1, Z):
            hz_arrival(h, (z + o) % Z).wait_recv()

        def one(r, carry):
            x = dot(placing(), hr[h, r].reshape(LANES, HALF))
            first = iota((LANES, HALF), 0) % 2 == 0
            left = jnp.where(first, x, 0.0).astype(BF16)
            right = jnp.where(first, 0.0, x).astype(BF16)
            for s in range(W):
                at = pl.ds(pl.multiple_of(16 * (CAP * s + r), 16), 16)
                hm[h, at, :HALF] = left[16 * s : 16 * s + 16]
                hm[h, at, HALF:] = right[16 * s : 16 * s + 16]
            return carry

        lax.fori_loop(0, CAP, one, 0)

    def y_copy(i, t):
        return remote(
            yb.at[i, :, pl.ds(pl.multiple_of(16 * t, 16), 16)],
            rx.at[i, pl.ds(CAP * w, CAP)],
            y_ss.at[i, t],
            y_rs.at[i, w],
            w_peer(t),
        )

    def y_arrival(i, s):
        at = pl.ds(CAP * s, CAP)
        return remote(rx.at[i, at], rx.at[i, at], y_ss.at[i, s], y_rs.at[i, s], w_peer(s))

    def gather_piece(i):
        for way in range(2):
            ag_arrival(i, way, hops(i, way) - 1).wait_recv()

        def one(n, carry):
            pick = pa[pl.ds(3 * n, 3)].reshape(3 * LANES, Z * TOK)
            yb[i, pl.ds(3 * n, 3)] = dot(pick, ga[i].reshape(Z * TOK, PC)).astype(BF16).reshape(3, LANES, PC)
            return carry

        lax.fori_loop(0, 3, one, 0)
        for o in range(1, W):
            y_copy(i, (w + o) % W).start()
        rx[i, pl.ds(CAP * w, CAP)] = yb[i, :, pl.ds(pl.multiple_of(16 * w, 16), 16)]

    def unit_of(i, j):
        u = 2 * piece_of(i) + j
        return u // 3, u % 3

    def rs_copy(i, h, j):
        owner, at = unit_of(i, j)
        return remote(
            su.at[h, 2 * i + j], rs.at[h, at, dp], rs_ss.at[h, 2 * i + j], rs_rs.at[h, at, dp], {"dp": owner}
        )

    def rs_arrival(h, at, s):
        return remote(su.at[h, 0], rs.at[h, at, s], rs_ss.at[h, 0], rs_rs.at[h, at, s], {"dp": s})

    def rows_piece(i):
        for o in range(1, W):
            y_arrival(i, (w + o) % W).wait_recv()
        for m in range(CAP):
            xt[i, :, m * LANES : (m + 1) * LANES] = rx[i, 8 * m : 8 * m + 8].reshape(LANES, PC).T

    def product_piece(i, h):
        def one(n, carry):
            at = pl.ds(pl.multiple_of(n * 256, 256), 256)
            out = dot(xt[i], hm[h, :, at]).astype(BF16)
            su[h, 2 * i, :, at] = out[:UNIT]
            su[h, 2 * i + 1, :, at] = out[UNIT:]
            return carry

        lax.fori_loop(0, 2, one, 0)
        for j in range(2):
            owner, at = unit_of(i, j)

            @pl.when(owner != dp)
            def _():
                rs_copy(i, h, j).start()

            @pl.when(owner == dp)
            def _():
                rs[h, at, dp] = su[h, 2 * i + j]

    make_tables()
    hidden_first()
    hidden_sort()
    attend_block()
    all_here()
    send_tables()
    attend_send()
    hidden_send(0)
    hidden_send(1)
    start_piece(0)
    start_piece(1)
    start_piece(2)
    weights_plane()
    forward(0, 1)
    forward(1, 1)
    forward(2, 1)
    attend_plane()
    forward(0, 2)
    forward(1, 2)
    forward(2, 2)
    forward(0, 3)
    forward(1, 3)
    forward(2, 3)
    hidden_plane(0)
    attend_carry()
    gather_piece(0)
    hidden_plane(1)
    start_piece(3)
    gather_piece(1)
    gather_piece(2)
    attend_last()
    start_piece(4)
    forward(3, 1)
    hidden_wide(0)
    rows_piece(0)
    product_piece(0, 0)
    forward(3, 2)
    start_piece(5)
    forward(4, 1)
    rows_piece(1)
    product_piece(1, 0)
    forward(3, 3)
    forward(4, 2)
    forward(5, 1)
    hidden_wide(1)
    product_piece(0, 1)
    product_piece(1, 1)
    rows_piece(2)
    product_piece(2, 0)
    product_piece(2, 1)
    gather_piece(3)
    forward(4, 3)
    forward(5, 2)
    gather_piece(4)
    forward(5, 3)
    gather_piece(5)
    rows_piece(3)
    product_piece(3, 0)
    product_piece(3, 1)
    rows_piece(4)
    product_piece(4, 0)
    product_piece(4, 1)
    rows_piece(5)
    product_piece(5, 0)
    product_piece(5, 1)

    for h in range(2):
        for at in range(3):
            for o in range(1, DP):
                rs_arrival(h, at, (dp + o) % DP).wait_recv()
            for e in range(2):
                cols = slice(e * HALF, (e + 1) * HALF)
                total = (rs[h, at, 0, :, cols].astype(F32) + rs[h, at, 1, :, cols].astype(F32)) + (
                    rs[h, at, 2, :, cols].astype(F32) + rs[h, at, 3, :, cols].astype(F32)
                )
                dg_ref[e, at * UNIT : (at + 1) * UNIT, h * HALF : (h + 1) * HALF] = total.astype(BF16)

    for i in range(PIECES):
        for way in range(2):
            for step in range(hops(i, way)):
                ag_copy(i, way, step).wait_send()
        for o in range(1, W):
            y_copy(i, (w + o) % W).wait_send()
        for j in range(2):
            @pl.when(unit_of(i, j)[0] != dp)
            def _():
                for h in range(2):
                    rs_copy(i, h, j).wait_send()
    for o in range(1, Z):
        t_copy((z + o) % Z).wait_send()
        for h in range(2):
            hz_copy(h, (z + o) % Z).wait_send()
            hw_copy(h, (w + o) % W).wait_send()
        a_copy((w + o) % W).wait_send()
        c_copy((w + o) % W).wait_send()
    for t in range(Z - 1):
        @pl.when(t < z)
        def _():
            b_copy(t).wait_send()


def on_device(saved_pre, layer_grad, router_weight, routes, queries, key_vectors, value_vectors, head_grad, log_gate):
    vmem = pl.BlockSpec(memory_space=pltpu.VMEM)
    dma = pltpu.SemaphoreType.DMA
    key_grad, value_grad, down_grad = pl.pallas_call(
        kernel,
        out_shape=(
            jax.ShapeDtypeStruct((TOK, 1024), BF16),
            jax.ShapeDtypeStruct((TOK, 1024), BF16),
            jax.ShapeDtypeStruct((2, OWN, FF), BF16),
        ),
        in_specs=[vmem] * 9,
        out_specs=(vmem, vmem, vmem),
        scratch_shapes=[
            pltpu.VMEM((PIECES, Z, TOK, PC), BF16),
            pltpu.VMEM((PAIRS, FF), BF16),
            pltpu.VMEM((2, CAP, LANES, HALF), BF16),
            pltpu.VMEM((2, CAP, W, 16, HALF), BF16),
            pltpu.VMEM((CAP, LANES, Z * TOK), BF16),
            pltpu.VMEM((2, CAP, LANES, HALF), BF16),
            pltpu.VMEM((2, CAP, Z, 16, HALF), BF16),
            pltpu.VMEM((2, W * CAP * 16, FF), BF16),
            pltpu.VMEM((PIECES, CAP, LANES, PC), BF16),
            pltpu.VMEM((PIECES, W * CAP, 16, PC), BF16),
            pltpu.VMEM((PIECES, PC, W * CAP * 16), BF16),
            pltpu.VMEM((2, 12, UNIT, FF), BF16),
            pltpu.VMEM((2, 3, DP, UNIT, FF), BF16),
            pltpu.VMEM((64, LANES), F32),
            pltpu.VMEM((TOK, 1024), F32),
            pltpu.VMEM((2 * TOP, TOK), F32),
            pltpu.VMEM((Z, 2 * TOP, TOK), F32),
            pltpu.VMEM((2 * LANES, TOK), F32),
            pltpu.VMEM((W, 72, LANES), F32),
            pltpu.VMEM((W, 72, LANES), F32),
            pltpu.VMEM((72, LANES), F32),
            pltpu.VMEM((Z, 72, LANES), F32),
            pltpu.VMEM((W, LANES, LANES), F32),
            pltpu.VMEM((W, 64, LANES), F32),
            pltpu.VMEM((W, 64, LANES), F32),
            dma((PIECES, 2, 4)),
            dma((PIECES, 2, 4)),
            dma((Z,)),
            dma((Z,)),
            dma((2, Z)),
            dma((2, Z)),
            dma((2, W)),
            dma((2, W)),
            dma((PIECES, W)),
            dma((PIECES, W)),
            dma((2, 12)),
            dma((2, 3, DP)),
            dma((W,)),
            dma((W,)),
            dma((Z,)),
            dma((Z,)),
            dma((W,)),
            dma((W,)),
        ],
        compiler_params=pltpu.CompilerParams(
            collective_id=0, has_side_effects=True, vmem_limit_bytes=60 * 1024 * 1024
        ),
        cost_estimate=pl.CostEstimate(flops=16_000_000_000, bytes_accessed=8_000_000, transcendentals=1_000_000),
    )(
        saved_pre,
        layer_grad,
        routes.T,
        router_weight.T,
        queries[0],
        key_vectors[0],
        value_vectors[0],
        head_grad[0],
        log_gate[0],
    )
    return key_grad[None], value_grad[None], jnp.swapaxes(down_grad, 1, 2)


def solution(mesh):
    return jax.shard_map(
        on_device,
        mesh=mesh,
        in_specs=(
            P(("dp", "ctx"), None, None),
            P(("dp", "ctx"), None),
            P(("dp", "ctx"), None),
            P(("dp", "ctx"), None),
            P("dp", "ctx", None),
            P("dp", "ctx", None),
            P("dp", "ctx", None),
            P("dp", "ctx", None),
            P("dp", "ctx", None),
        ),
        out_specs=(P("dp", "ctx", None), P("dp", "ctx", None), P("ctx", None, "dp")),
        check_vma=False,
    )
```

```python
import functools

import jax
import jax.numpy as jnp
from jax import lax
from jax.experimental import pallas as pl
from jax.experimental.pallas import tpu as pltpu
from jax.sharding import PartitionSpec as P

FF = 512
HALF = FF // 2
TOK = 128
D = 2304
Z = 8
W = 8
DP = 4
CAP = 9
TOP = 8
PAIRS = TOK * TOP
PIECES = 6
PC = D // PIECES
UNIT = D // 12
OWN = D // DP
LANES = 128
MESH = pl.DeviceIdType.MESH
F32 = jnp.float32
BF16 = jnp.bfloat16


def iota(shape, dim):
    return lax.broadcasted_iota(jnp.int32, shape, dim)


def dot(a, b):
    return lax.dot_general(a, b, (((1,), (0,)), ((), ())), preferred_element_type=F32)


def dot_nt(a, b):
    return lax.dot_general(a, b, (((1,), (1,)), ((), ())), preferred_element_type=F32)


def dot_tn(a, b):
    return lax.dot_general(a, b, (((0,), (0,)), ((), ())), preferred_element_type=F32)


def split2(x):
    hi = x.astype(BF16)
    return hi, (x - hi.astype(F32)).astype(BF16)


def kernel(
    pre_ref, g_ref, rt_ref, wt_ref, q_ref, k_ref, v_ref, do_ref, lg_ref,
    kg_ref, vg_ref, dg_ref,
    ga, hid, sh, hin, pa, hy, hr, hm, yb, rx, xt, su, rs, acc,
    cum, tb_s, tb_r, pt, a_s, a_r, b_s, b_r, cl, c_s, c_r,
    ag_ss, ag_rs, t_ss, t_rs, hz_ss, hz_rs, hw_ss, hw_rs, y_ss, y_rs, rs_ss, rs_rs,
    a_ss, a_rs, b_ss, b_rs, c_ss, c_rs,
):
    dp = lax.axis_index("dp")
    ctx = lax.axis_index("ctx")
    z = ctx // W
    w = ctx % W

    def z_peer(t):
        return {"ctx": t * W + w}

    def w_peer(t):
        return {"ctx": z * W + t}

    def remote(src, dst, ss, rsem, dev):
        return pltpu.make_async_remote_copy(
            src_ref=src, dst_ref=dst, send_sem=ss, recv_sem=rsem, device_id=dev, device_id_type=MESH
        )

    barrier = pltpu.get_barrier_semaphore()
    for o in range(1, Z):
        pl.semaphore_signal(barrier, inc=1, device_id=z_peer((z + o) % Z), device_id_type=MESH)
        pl.semaphore_signal(barrier, inc=1, device_id=w_peer((w + o) % W), device_id_type=MESH)
    for o in range(1, DP):
        pl.semaphore_signal(barrier, inc=1, device_id={"dp": (dp + o) % DP}, device_id_type=MESH)

    def all_here():
        pl.semaphore_wait(barrier, (Z - 1) + (W - 1) + (DP - 1))

    first_piece = (2 + (3 * dp) // 2) % PIECES

    def piece_of(i):
        return (first_piece + i) % PIECES

    def hops(i, way):
        return 4 if (i % 2 == 0) == (way == 0) else 3

    def ag_copy(i, way, step):
        src = (z - step + Z) % Z if way == 0 else (z + step) % Z
        to = (z + 1) % Z if way == 0 else (z + Z - 1) % Z
        return remote(ga.at[i, src], ga.at[i, src], ag_ss.at[i, way, step], ag_rs.at[i, way, step], z_peer(to))

    def ag_arrival(i, way, step):
        src = (z - 1 - step + 2 * Z) % Z if way == 0 else (z + 1 + step) % Z
        return remote(
            ga.at[i, src], ga.at[i, src], ag_ss.at[i, way, step], ag_rs.at[i, way, step], z_peer((z + 1) % Z)
        )

    def start_piece(i):
        ga[i, z] = g_ref[:, pl.ds(pl.multiple_of(piece_of(i) * PC, LANES), PC)]
        ag_copy(i, 0, 0).start()
        ag_copy(i, 1, 0).start()

    def forward(i, step):
        for way in range(2):
            if step < hops(i, way):
                ag_arrival(i, way, step - 1).wait_recv()
                ag_copy(i, way, step).start()

    def t_copy(t):
        return remote(tb_s, tb_r.at[z], t_ss.at[t], t_rs.at[z], z_peer(t))

    def t_arrival(s):
        return remote(tb_s, tb_r.at[s], t_ss.at[s], t_rs.at[s], z_peer(s))

    def make_tables():
        tb_s[:TOP] = rt_ref[...].astype(F32)
        tb_s[TOP:] = wt_ref[...].astype(F32)

    def send_tables():
        for o in range(1, Z):
            t_copy((z + o) % Z).start()
        tb_r[z] = tb_s[...]

    before = jnp.where(iota((TOK, TOK), 0) < iota((TOK, TOK), 1), 1.0, 0.0).astype(BF16)

    def hidden_first():
        def hidden_block(n, carry):
            x = pre_ref[pl.ds(n * 16, 16)].astype(F32).reshape(LANES, 2 * FF)
            gate, up = x[:, :FF], x[:, FF:]
            hid[pl.ds(pl.multiple_of(n * LANES, LANES), LANES), :] = (gate / (1.0 + jnp.exp(-gate)) * up).astype(BF16)
            return carry

        lax.fori_loop(0, PAIRS // LANES, hidden_block, 0)

    def expert_at(shape):
        row = iota(shape, 0)
        return (row // 2) % 8 * 16 + row // 16 * 2 + row % 2

    def hidden_sort():
        expert = expert_at((LANES, TOK)).astype(F32)
        by_token = jnp.zeros((LANES, TOK), F32)
        for j in range(TOP):
            by_token = by_token + jnp.where(tb_s[j : j + 1] == expert, 1.0, 0.0)
        rank = dot(by_token.astype(BF16), before)
        rank = jnp.where(by_token > 0.5, rank, -1.0)
        token_of = jnp.where(iota((PAIRS, TOK), 0) // TOP == iota((PAIRS, TOK), 1), 1.0, 0.0).astype(BF16)
        wide = dot_nt(tb_s[:TOP].astype(BF16), token_of)
        chosen = iota((TOP, PAIRS), 0) == iota((TOP, PAIRS), 1) % TOP
        route = jnp.sum(jnp.where(chosen, wide, 0.0), axis=0, keepdims=True)
        rank_pair = jnp.where(route == expert_at((LANES, PAIRS)).astype(F32), dot_nt(rank.astype(BF16), token_of), -1.0)
        for r in range(CAP):
            pa[r] = jnp.where(rank_pair == float(r), 1.0, 0.0).astype(BF16)

        def sort_block(n, carry):
            pick = pa[pl.ds(3 * n, 3)].reshape(3 * LANES, PAIRS)
            x = dot(pick, hid[...]).astype(BF16)
            sh[0, pl.ds(3 * n, 3)] = x[:, :HALF].reshape(3, LANES, HALF)
            sh[1, pl.ds(3 * n, 3)] = x[:, HALF:].reshape(3, LANES, HALF)
            return carry

        lax.fori_loop(0, 3, sort_block, 0)

    def hw_copy(h, t):
        at = pl.ds(pl.multiple_of(16 * t, 16), 16)
        return remote(sh.at[h, :, at], hin.at[h, :, w], hw_ss.at[h, t], hw_rs.at[h, w], w_peer(t))

    def hw_arrival(h, s):
        return remote(hin.at[h, :, w], hin.at[h, :, s], hw_ss.at[h, s], hw_rs.at[h, s], w_peer(s))

    def hidden_send(h):
        for o in range(1, W):
            hw_copy(h, (w + o) % W).start()
        hin[h, :, w] = sh[h, :, pl.ds(pl.multiple_of(16 * w, 16), 16)]

    lane = iota((LANES, LANES), 1)
    low = lane < 64
    low64 = iota((64, LANES), 1) < 64
    tri = jnp.where(iota((TOK, TOK), 1) <= iota((TOK, TOK), 0), 1.0, 0.0).astype(BF16)

    def attend_first(j, carry):
        at = pl.ds(pl.multiple_of(j * LANES, LANES), LANES)
        x = lg_ref[:, at]
        hi, rest = split2(x)
        mid, lo = split2(x - hi.astype(F32))
        total = dot(tri, hi) + (dot(tri, mid) + dot(tri, lo))
        cum[:, at] = total
        qh, ql = split2(q_ref[:, at].astype(F32) * jnp.exp(total))
        do = do_ref[:, at]
        s = dot_tn(qh, do) + dot_tn(ql, do)
        a_s[j, :64] = jnp.where(low64, s[:64], s[64:])
        a_s[j, 64:] = jnp.broadcast_to(total[TOK - 1 :], (8, LANES))
        return carry

    def a_copy(t):
        return remote(a_s.at[t], a_r.at[w], a_ss.at[t], a_rs.at[w], w_peer(t))

    def a_arrival(s):
        return remote(a_s.at[s], a_r.at[s], a_ss.at[s], a_rs.at[s], w_peer(s))

    def attend_block():
        lax.fori_loop(0, W, attend_first, 0)

    def attend_send():
        for o in range(1, W):
            a_copy((w + o) % W).start()
        a_r[w] = a_s[w]

    def down_channels(row):
        x = jnp.broadcast_to(row, (LANES, LANES)).T
        return jnp.where(low64, x[:64], x[64:])

    def b_copy(t):
        return remote(b_s, b_r.at[z], b_ss.at[t], b_rs.at[z], z_peer(t))

    def b_arrival(s):
        return remote(b_s, b_r.at[s], b_ss.at[s], b_rs.at[s], z_peer(s))

    def attend_plane():
        for o in range(1, W):
            a_arrival((w + o) % W).wait_recv()
        c = jnp.zeros((64, LANES), F32)
        d = jnp.zeros((64, LANES), F32)
        whole = jnp.zeros((8, LANES), F32)
        for b in range(W - 1, -1, -1):
            cl[b, :64] = c
            cl[b, 64:] = d
            ld = down_channels(a_r[b, 64:65])
            c = a_r[b, :64] + jnp.exp(ld) * c
            d = d + ld
            whole = whole + a_r[b, 64:]
        b_s[:64] = c
        b_s[64:] = whole
        for t in range(Z - 1):
            @pl.when(t < z)
            def _():
                b_copy(t).start()

    def c_copy(t):
        return remote(c_s.at[t], c_r.at[w], c_ss.at[t], c_rs.at[w], w_peer(t))

    def c_arrival(s):
        return remote(c_s.at[s], c_r.at[s], c_ss.at[s], c_rs.at[s], w_peer(s))

    def attend_carry():
        acc[...] = jnp.zeros((64, LANES), F32)
        for s in range(Z - 1, 0, -1):
            @pl.when(s > z)
            def _():
                b_arrival(s).wait_recv()
                acc[...] = b_r[s, :64] + jnp.exp(down_channels(b_r[s, 64:65])) * acc[...]
        x = acc[...]
        for b in range(W):
            c_s[b] = cl[b, :64] + jnp.exp(cl[b, 64:]) * x
        for o in range(1, W):
            c_copy((w + o) % W).start()
        c_r[w] = c_s[w]

    def attend_last():
        for o in range(1, W):
            c_arrival((w + o) % W).wait_recv()
        later = iota((TOK, TOK), 0) <= iota((TOK, TOK), 1)

        def pair(j, carry):
            at = pl.ds(pl.multiple_of(j * LANES, LANES), LANES)
            total = cum[:, at]
            middle = total[63:64]
            ek = jnp.exp(middle - total)
            tail = jnp.exp(total[TOK - 1 :] - total)
            k = k_ref[:, at].astype(F32)
            v = v_ref[:, at]
            do = do_ref[:, at]
            qs = q_ref[:, at].astype(F32) * jnp.exp(total - middle)
            ks = k * ek
            qh, ql = split2(qs)
            vo = jnp.zeros((TOK, LANES), F32)
            ko = jnp.zeros((TOK, LANES), F32)
            for half in (low, jnp.logical_not(low)):
                kh, kl = split2(jnp.where(half, ks, 0.0))
                scores = dot_nt(kh, qh) + (dot_nt(kh, ql) + dot_nt(kl, qh))
                sh_, sl_ = split2(jnp.where(later, scores, 0.0))
                dom = jnp.where(half, do.astype(F32), 0.0).astype(BF16)
                vo = vo + (dot(sh_, dom) + dot(sl_, dom))
                vm = jnp.where(half, v.astype(F32), 0.0).astype(BF16)
                bh, bl = split2(jnp.where(later, dot_nt(vm, do), 0.0))
                qmh, qml = split2(jnp.where(half, qs, 0.0))
                ko = ko + (dot(bh, qmh) + (dot(bl, qmh) + dot(bh, qml)))
            c = c_r[j]
            ch, clo = split2(jnp.concatenate([jnp.where(low64, c, 0.0), jnp.where(low64, 0.0, c)], axis=0))
            th, tl = split2(k * tail)
            vo = vo + (dot(th, ch) + (dot(th, clo) + dot(tl, ch)))
            ko = ek * ko + tail * (dot_nt(v, ch) + dot_nt(v, clo))
            kg_ref[:, at] = ko.astype(BF16)
            vg_ref[:, at] = vo.astype(BF16)
            return carry

        lax.fori_loop(0, W, pair, 0)

    def hz_copy(h, t):
        at = pl.ds(pl.multiple_of(16 * t, 16), 16)
        return remote(hy.at[h, :, at], hr.at[h, :, z], hz_ss.at[h, t], hz_rs.at[h, z], z_peer(t))

    def hz_arrival(h, s):
        return remote(hr.at[h, :, z], hr.at[h, :, s], hz_ss.at[h, s], hz_rs.at[h, s], z_peer(s))

    def placing():
        row = iota((LANES, LANES), 0)
        col = iota((LANES, LANES), 1)
        same = (row // 2) % 8 == col // 16
        return jnp.where(same & (col % 16 == 2 * (row // 16) + row % 2), 1.0, 0.0).astype(BF16)

    def weights_plane():
        for o in range(1, Z):
            t_arrival((z + o) % Z).wait_recv()
        expert = (iota((16, TOK), 0) + 16 * z).astype(F32)
        for s in range(Z):
            count = jnp.zeros((16, TOK), F32)
            weight = jnp.zeros((16, TOK), F32)
            for j in range(TOP):
                hit = tb_r[s, j : j + 1] == expert
                count = count + jnp.where(hit, 1.0, 0.0)
                weight = weight + jnp.where(hit, tb_r[s, TOP + j : TOP + j + 1], 0.0)
            pt[16 * s : 16 * s + 16] = count
            pt[LANES + 16 * s : LANES + 16 * s + 16] = weight
        count = pt[:LANES]
        rank = jnp.where(count > 0.5, dot(count.astype(BF16), before), -1.0)
        rank = dot(placing(), rank.astype(BF16))
        weight = dot(placing(), pt[LANES:].astype(BF16))
        source = (iota((LANES, TOK), 0) // 2) % Z
        for r in range(CAP):
            mine = jnp.where(rank == float(r), weight, 0.0)
            for s in range(Z):
                pa[r, :, s * LANES : (s + 1) * LANES] = jnp.where(source == s, mine, 0.0).astype(BF16)

    def hidden_plane(h):
        for o in range(1, W):
            hw_arrival(h, (w + o) % W).wait_recv()

        def one(r, carry):
            hy[h, r] = dot(placing(), hin[h, r].reshape(LANES, HALF)).astype(BF16)
            return carry

        lax.fori_loop(0, CAP, one, 0)
        for o in (4, 3, 5, 2, 6, 1, 7):
            hz_copy(h, (z + o) % Z).start()
        hr[h, :, z] = hy[h, :, pl.ds(pl.multiple_of(16 * z, 16), 16)]

    def hidden_wide(h):
        for o in range(1, Z):
            hz_arrival(h, (z + o) % Z).wait_recv()

        def one(r, carry):
            x = dot(placing(), hr[h, r].reshape(LANES, HALF))
            first = iota((LANES, HALF), 0) % 2 == 0
            left = jnp.where(first, x, 0.0).astype(BF16)
            right = jnp.where(first, 0.0, x).astype(BF16)
            for s in range(W):
                at = pl.ds(pl.multiple_of(16 * (CAP * s + r), 16), 16)
                hm[h, at, :HALF] = left[16 * s : 16 * s + 16]
                hm[h, at, HALF:] = right[16 * s : 16 * s + 16]
            return carry

        lax.fori_loop(0, CAP, one, 0)

    def y_copy(i, t):
        return remote(
            yb.at[i, :, pl.ds(pl.multiple_of(16 * t, 16), 16)],
            rx.at[i, pl.ds(CAP * w, CAP)],
            y_ss.at[i, t],
            y_rs.at[i, w],
            w_peer(t),
        )

    def y_arrival(i, s):
        at = pl.ds(CAP * s, CAP)
        return remote(rx.at[i, at], rx.at[i, at], y_ss.at[i, s], y_rs.at[i, s], w_peer(s))

    def gather_piece(i):
        for way in range(2):
            ag_arrival(i, way, hops(i, way) - 1).wait_recv()

        def one(n, carry):
            pick = pa[pl.ds(3 * n, 3)].reshape(3 * LANES, Z * TOK)
            yb[i, pl.ds(3 * n, 3)] = dot(pick, ga[i].reshape(Z * TOK, PC)).astype(BF16).reshape(3, LANES, PC)
            return carry

        lax.fori_loop(0, 3, one, 0)
        for o in range(1, W):
            y_copy(i, (w + o) % W).start()
        rx[i, pl.ds(CAP * w, CAP)] = yb[i, :, pl.ds(pl.multiple_of(16 * w, 16), 16)]

    def unit_of(i, j):
        u = 2 * piece_of(i) + j
        return u // 3, u % 3

    def rs_copy(i, h, j):
        owner, at = unit_of(i, j)
        return remote(
            su.at[h, 2 * i + j], rs.at[h, at, dp], rs_ss.at[h, 2 * i + j], rs_rs.at[h, at, dp], {"dp": owner}
        )

    def rs_arrival(h, at, s):
        return remote(su.at[h, 0], rs.at[h, at, s], rs_ss.at[h, 0], rs_rs.at[h, at, s], {"dp": s})

    def rows_piece(i):
        for o in range(1, W):
            y_arrival(i, (w + o) % W).wait_recv()
        for m in range(CAP):
            xt[i, :, m * LANES : (m + 1) * LANES] = rx[i, 8 * m : 8 * m + 8].reshape(LANES, PC).T

    def product_piece(i, h):
        def one(n, carry):
            at = pl.ds(pl.multiple_of(n * 256, 256), 256)
            out = dot(xt[i], hm[h, :, at]).astype(BF16)
            su[h, 2 * i, :, at] = out[:UNIT]
            su[h, 2 * i + 1, :, at] = out[UNIT:]
            return carry

        lax.fori_loop(0, 2, one, 0)
        for j in range(2):
            owner, at = unit_of(i, j)

            @pl.when(owner != dp)
            def _():
                rs_copy(i, h, j).start()

            @pl.when(owner == dp)
            def _():
                rs[h, at, dp] = su[h, 2 * i + j]

    make_tables()
    hidden_first()
    hidden_sort()
    attend_block()
    all_here()
    send_tables()
    attend_send()
    hidden_send(0)
    hidden_send(1)
    start_piece(0)
    start_piece(1)
    start_piece(2)
    weights_plane()
    forward(0, 1)
    forward(1, 1)
    forward(2, 1)
    attend_plane()
    forward(0, 2)
    forward(1, 2)
    forward(2, 2)
    forward(0, 3)
    forward(1, 3)
    forward(2, 3)
    hidden_plane(0)
    attend_carry()
    gather_piece(0)
    hidden_plane(1)
    gather_piece(1)
    start_piece(3)
    attend_last()
    hidden_wide(0)
    rows_piece(0)
    product_piece(0, 0)
    forward(3, 1)
    start_piece(4)
    gather_piece(2)
    rows_piece(1)
    product_piece(1, 0)
    forward(3, 2)
    forward(4, 1)
    hidden_wide(1)
    product_piece(0, 1)
    product_piece(1, 1)
    start_piece(5)
    forward(3, 3)
    forward(4, 2)
    forward(5, 1)
    gather_piece(3)
    rows_piece(2)
    product_piece(2, 0)
    product_piece(2, 1)
    forward(4, 3)
    forward(5, 2)
    gather_piece(4)
    forward(5, 3)
    rows_piece(3)
    product_piece(3, 0)
    product_piece(3, 1)
    gather_piece(5)
    rows_piece(4)
    product_piece(4, 0)
    product_piece(4, 1)
    rows_piece(5)
    product_piece(5, 0)
    product_piece(5, 1)

    for h in range(2):
        for at in range(3):
            for o in range(1, DP):
                rs_arrival(h, at, (dp + o) % DP).wait_recv()
            for e in range(2):
                cols = slice(e * HALF, (e + 1) * HALF)
                total = (rs[h, at, 0, :, cols].astype(F32) + rs[h, at, 1, :, cols].astype(F32)) + (
                    rs[h, at, 2, :, cols].astype(F32) + rs[h, at, 3, :, cols].astype(F32)
                )
                dg_ref[e, at * UNIT : (at + 1) * UNIT, h * HALF : (h + 1) * HALF] = total.astype(BF16)

    for i in range(PIECES):
        for way in range(2):
            for step in range(hops(i, way)):
                ag_copy(i, way, step).wait_send()
        for o in range(1, W):
            y_copy(i, (w + o) % W).wait_send()
        for j in range(2):
            @pl.when(unit_of(i, j)[0] != dp)
            def _():
                for h in range(2):
                    rs_copy(i, h, j).wait_send()
    for o in range(1, Z):
        t_copy((z + o) % Z).wait_send()
        for h in range(2):
            hz_copy(h, (z + o) % Z).wait_send()
            hw_copy(h, (w + o) % W).wait_send()
        a_copy((w + o) % W).wait_send()
        c_copy((w + o) % W).wait_send()
    for t in range(Z - 1):
        @pl.when(t < z)
        def _():
            b_copy(t).wait_send()


def on_device(saved_pre, layer_grad, router_weight, routes, queries, key_vectors, value_vectors, head_grad, log_gate):
    vmem = pl.BlockSpec(memory_space=pltpu.VMEM)
    dma = pltpu.SemaphoreType.DMA
    key_grad, value_grad, down_grad = pl.pallas_call(
        kernel,
        out_shape=(
            jax.ShapeDtypeStruct((TOK, 1024), BF16),
            jax.ShapeDtypeStruct((TOK, 1024), BF16),
            jax.ShapeDtypeStruct((2, OWN, FF), BF16),
        ),
        in_specs=[vmem] * 9,
        out_specs=(vmem, vmem, vmem),
        scratch_shapes=[
            pltpu.VMEM((PIECES, Z, TOK, PC), BF16),
            pltpu.VMEM((PAIRS, FF), BF16),
            pltpu.VMEM((2, CAP, LANES, HALF), BF16),
            pltpu.VMEM((2, CAP, W, 16, HALF), BF16),
            pltpu.VMEM((CAP, LANES, Z * TOK), BF16),
            pltpu.VMEM((2, CAP, LANES, HALF), BF16),
            pltpu.VMEM((2, CAP, Z, 16, HALF), BF16),
            pltpu.VMEM((2, W * CAP * 16, FF), BF16),
            pltpu.VMEM((PIECES, CAP, LANES, PC), BF16),
            pltpu.VMEM((PIECES, W * CAP, 16, PC), BF16),
            pltpu.VMEM((PIECES, PC, W * CAP * 16), BF16),
            pltpu.VMEM((2, 12, UNIT, FF), BF16),
            pltpu.VMEM((2, 3, DP, UNIT, FF), BF16),
            pltpu.VMEM((64, LANES), F32),
            pltpu.VMEM((TOK, 1024), F32),
            pltpu.VMEM((2 * TOP, TOK), F32),
            pltpu.VMEM((Z, 2 * TOP, TOK), F32),
            pltpu.VMEM((2 * LANES, TOK), F32),
            pltpu.VMEM((W, 72, LANES), F32),
            pltpu.VMEM((W, 72, LANES), F32),
            pltpu.VMEM((72, LANES), F32),
            pltpu.VMEM((Z, 72, LANES), F32),
            pltpu.VMEM((W, LANES, LANES), F32),
            pltpu.VMEM((W, 64, LANES), F32),
            pltpu.VMEM((W, 64, LANES), F32),
            dma((PIECES, 2, 4)),
            dma((PIECES, 2, 4)),
            dma((Z,)),
            dma((Z,)),
            dma((2, Z)),
            dma((2, Z)),
            dma((2, W)),
            dma((2, W)),
            dma((PIECES, W)),
            dma((PIECES, W)),
            dma((2, 12)),
            dma((2, 3, DP)),
            dma((W,)),
            dma((W,)),
            dma((Z,)),
            dma((Z,)),
            dma((W,)),
            dma((W,)),
        ],
        compiler_params=pltpu.CompilerParams(
            collective_id=0, has_side_effects=True, vmem_limit_bytes=60 * 1024 * 1024
        ),
        cost_estimate=pl.CostEstimate(flops=16_000_000_000, bytes_accessed=8_000_000, transcendentals=1_000_000),
    )(
        saved_pre,
        layer_grad,
        routes.T,
        router_weight.T,
        queries[0],
        key_vectors[0],
        value_vectors[0],
        head_grad[0],
        log_gate[0],
    )
    return key_grad[None], value_grad[None], jnp.swapaxes(down_grad, 1, 2)


def solution(mesh):
    return jax.shard_map(
        on_device,
        mesh=mesh,
        in_specs=(
            P(("dp", "ctx"), None, None),
            P(("dp", "ctx"), None),
            P(("dp", "ctx"), None),
            P(("dp", "ctx"), None),
            P("dp", "ctx", None),
            P("dp", "ctx", None),
            P("dp", "ctx", None),
            P("dp", "ctx", None),
            P("dp", "ctx", None),
        ),
        out_specs=(P("dp", "ctx", None), P("dp", "ctx", None), P("ctx", None, "dp")),
        check_vma=False,
    )
```
